256 devices in a mesh: rows: 4 (over x), chan: 8 (over y, z_lo), filt: 8 (over z_hi, core).
Axes of the slice: x: 4, y: 4, z: 8 (z_hi: 4, z_lo: 2; z = z_hi * 2 + z_lo), core: 2. Of those that a mesh axis runs over, the one named last changes fastest.
Arguments:
- images: bfloat16 [16, 2048, 2048], P('rows', 'chan', 'filt'), may hold values from -6 to 6
- first_weight: bfloat16 [2048, 1024], P('chan', 'filt'), may hold values from -0.125 to 0.125
- group_weight: bfloat16 [3, 3, 32, 1024], P(None, None, None, 'filt'), may hold values from -0.375 to 0.375
- third_weight: bfloat16 [1024, 2048], P('chan', 'filt'), may hold values from -0.1875 to 0.1875
- out_grad: bfloat16 [16, 2048, 2048], P('rows', 'chan', 'filt'), may hold values from -6 to 6
Outputs:
- block_out: bfloat16 [16, 2048, 2048], P('rows', 'chan', 'filt')
- images_grad: float32 [16, 2048, 2048], P('rows', 'chan', 'filt')
- first_grad: float32 [2048, 1024], P('chan', 'filt')
- group_grad: float32 [3, 3, 32, 1024], P(None, None, None, 'filt')
- third_grad: float32 [1024, 2048], P('chan', 'filt')
The draws below stay inside these ranges and needn't reach their ends.
All inputs are finite; a program needn't handle non-finite values.
Results may differ from the reference program's by a relative error of at most 0.006.
Values may be sent and summed in bfloat16 or wider, within the bound.
No kernel may reach another device: no remote copies, remote signals or barrier semaphores. Data moves between devices by JAX's collectives and lax.ppermute only.
A program may use at most 128 MiB of HBM per device.

```python
import jax
import jax.numpy as jnp
from jax import lax

C = 2048
MID = 1024
GS = 32
WD = 2048
H = 16
GROUPS = 32


def level_of(own_key, shape, split, low, top_value):
    def one(axis_at, blocks):
        draws = jax.random.uniform(jax.random.fold_in(jax.random.fold_in(own_key, 6), axis_at), (blocks,), jnp.float32, low / len(split), top_value / len(split))
        return jnp.repeat(jnp.exp(draws), shape[axis_at] // blocks).reshape((-1,) + (1,) * (len(shape) - axis_at - 1))

    loudness = one(*split[0])
    for cut in split[1:]:
        loudness = loudness * one(*cut)
    return loudness


def scatter_about(rng, shape, width, bound, shards=(), dtype=jnp.bfloat16):
    loudness = level_of(rng, shape, shards, -0.22, 0.18) if shards else 1.0
    values = jax.random.normal(rng, shape, jnp.float32) * width * loudness
    return jnp.minimum(jnp.maximum(values, -bound), bound).astype(dtype)


def setup_inputs(seed: int = 0) -> dict:
    arg_keys = jax.random.split(jax.random.key(seed), 6)
    return {
        "images": scatter_about(arg_keys[0], (H, WD, C), 1.0, 6.0, ((0, 4), (1, 8), (2, 8))),
        "first_weight": scatter_about(arg_keys[1], (C, MID), C ** -0.5, 0.125, ((0, 8), (1, 8))),
        "group_weight": scatter_about(arg_keys[2], (3, 3, GS, MID), (9 * GS) ** -0.5, 0.375, ((3, 8),)),
        "third_weight": scatter_about(arg_keys[3], (MID, C), MID ** -0.5, 0.1875, ((0, 8), (1, 8))),
        "out_grad": scatter_about(arg_keys[4], (H, WD, C), 1.0, 6.0, ((0, 4), (1, 8), (2, 8))),
    }


def silu_slope(values):
    logistic = jax.nn.sigmoid(values)
    return logistic * (1.0 + values * (1.0 - logistic))

def group_conv(values, kernel):
    result = lax.conv_general_dilated(values[None], kernel, (1, 1), 'SAME', dimension_numbers=('NHWC', 'HWIO', 'NHWC'), feature_group_count=GROUPS, precision=lax.Precision.HIGHEST)
    return result[0]

def reference(images, first_weight, group_weight, third_weight, out_grad):
    pixels = H * WD
    flat_images = images.reshape(pixels, C)
    pre_first = jnp.dot(flat_images, first_weight, preferred_element_type=jnp.float32)
    act_first = jax.nn.silu(pre_first).astype(jnp.bfloat16).reshape(H, WD, MID)
    kernel = group_weight.astype(jnp.float32)
    pre_group = group_conv(act_first.astype(jnp.float32), kernel)
    act_group = jax.nn.silu(pre_group).astype(jnp.bfloat16).reshape(pixels, MID)
    third_out = jnp.dot(act_group, third_weight, preferred_element_type=jnp.float32)
    block_out = (flat_images.astype(jnp.float32) + third_out).astype(jnp.bfloat16).reshape(H, WD, C)
    grad_flat = out_grad.reshape(pixels, C)
    mid_grad = lax.dot_general(grad_flat, third_weight, (((1,), (1,)), ((), ())), preferred_element_type=jnp.float32)
    third_grad = lax.dot_general(act_group, grad_flat, (((0,), (0,)), ((), ())), preferred_element_type=jnp.float32)
    group_delta = (mid_grad * silu_slope(pre_group.reshape(pixels, MID))).astype(jnp.bfloat16).reshape(H, WD, MID)
    unused, pullback = jax.vjp(group_conv, act_first.astype(jnp.float32), kernel)
    first_back, group_grad = pullback(group_delta.astype(jnp.float32))
    first_delta = (first_back.reshape(pixels, MID) * silu_slope(pre_first)).astype(jnp.bfloat16)
    first_grad = lax.dot_general(flat_images, first_delta, (((0,), (0,)), ((), ())), preferred_element_type=jnp.float32)
    back_images = lax.dot_general(first_delta, first_weight, (((1,), (1,)), ((), ())), preferred_element_type=jnp.float32)
    images_grad = (grad_flat.astype(jnp.float32) + back_images).reshape(H, WD, C)
    return (block_out, images_grad, first_grad, group_grad, third_grad)
```

```python
import jax
import jax.numpy as jnp
from jax import lax
from jax.experimental import pallas as pl
from jax.experimental.pallas import tpu as pltpu
from jax.sharding import PartitionSpec as P

F32 = jnp.float32
BF16 = jnp.bfloat16
VMEM = pl.BlockSpec(memory_space=pltpu.VMEM)
SMEM = pl.BlockSpec(memory_space=pltpu.SMEM)


def dot(a, b, ca=1, cb=0):
    return lax.dot_general(a, b, (((ca,), (cb,)), ((), ())), preferred_element_type=F32)


def call(kernel, outs, n_smem, args, scratch=()):
    return pl.pallas_call(
        kernel,
        out_shape=[jax.ShapeDtypeStruct(s, d) for s, d in outs],
        in_specs=[SMEM] * n_smem + [VMEM] * (len(args) - n_smem),
        out_specs=[VMEM] * len(outs),
        scratch_shapes=list(scratch),
        compiler_params=pltpu.CompilerParams(vmem_limit_bytes=48 * 2**20),
    )(*args)


def block_of(ref, zone, step, size):
    which = lax.rem(zone + step, 4)
    return ref[pl.ds(pl.multiple_of(which * size, size), size), :]


def logistic(v):
    return 1.0 / (1.0 + jnp.exp(-v))


def slope(v):
    s = logistic(v)
    return s * (1.0 + v * (1.0 - s))


def first_kernel(zone_ref, own, left, right, far_a, far_b, w1, pre, act):
    zone = zone_ref[0]
    half = far_a.shape[0]
    size = own.shape[1]
    for part, far in ((0, far_a), (1, far_b)):
        rows = pl.ds(part * half, half)
        v = dot(own[rows, :], block_of(w1, zone, 0, size))
        v += dot(left[rows, :], block_of(w1, zone, 3, size))
        v += dot(right[rows, :], block_of(w1, zone, 1, size))
        v += dot(far[...], block_of(w1, zone, 2, size))
        pre[rows, :] = v
        act[rows, :] = (v * logistic(v)).astype(BF16)


def mid_kernel(zone_ref, grad, w3, p0, p1, p3, p2):
    zone = zone_ref[0]
    size = p0.shape[1]
    g = grad[...]
    p2[...] = dot(g, block_of(w3, zone, 2, size), 1, 1).astype(BF16)
    p1[...] = dot(g, block_of(w3, zone, 1, size), 1, 1).astype(BF16)
    p3[...] = dot(g, block_of(w3, zone, 3, size), 1, 1).astype(BF16)
    p0[...] = dot(g, block_of(w3, zone, 0, size), 1, 1)


def shifted(rows_total, cols, up, mid, down, low, high, out):
    chans = mid.shape[1]
    x = jnp.concatenate([up[...].astype(F32), mid[...].astype(F32), down[...].astype(F32)], axis=0)
    n = rows_total * cols
    col = lax.rem(lax.broadcasted_iota(jnp.int32, (n, chans), 0), cols)

    def spread(edge):
        parts = [jnp.broadcast_to(edge[i : i + 1, :], (cols, chans)) for i in range(rows_total)]
        return jnp.concatenate(parts, axis=0)

    out[1] = x.astype(BF16)
    out[0] = jnp.where(col == 0, spread(low), pltpu.roll(x, 1, 0)).astype(BF16)
    out[2] = jnp.where(col == cols - 1, spread(high), pltpu.roll(x, n - 1, 0)).astype(BF16)


def group_kernel(up, mid, down, low, high, wd, pre, act, xs):
    n = mid.shape[0]
    cols = up.shape[0]
    shifted(n // cols + 2, cols, up, mid, down, low, high, xs)
    total = jnp.zeros(pre.shape, F32)
    for a in range(3):
        for b in range(3):
            total += dot(xs[b, a * cols : a * cols + n, :], wd[3 * a + b])
    pre[...] = total
    act[...] = (total * logistic(total)).astype(BF16)


def group_grad_kernel(xs, delta, out):
    n, chans = delta.shape
    cols = xs.shape[1] - n
    cols = cols // 2
    size = out.shape[1]
    d = delta[...]
    row_group = lax.broadcasted_iota(jnp.int32, (chans, chans), 0) // size
    col_group = lax.broadcasted_iota(jnp.int32, (chans, chans), 1) // size
    keep = row_group == col_group
    for a in range(3):
        for b in range(3):
            full = dot(xs[b, a * cols : a * cols + n, :], d, 0, 0)
            full = jnp.where(keep, full, 0.0)
            total = full[0:size]
            for g in range(1, chans // size):
                total += full[g * size : (g + 1) * size]
            out[3 * a + b] = total


def back_kernel(zone_ref, up, mid, down, low, high, wd, pre, w1, fdelta, p0, p1, p3, p2, ds):
    zone = zone_ref[0]
    n = mid.shape[0]
    cols = up.shape[0]
    shifted(n // cols + 2, cols, up, mid, down, low, high, ds)
    total = jnp.zeros(pre.shape, F32)
    for a in range(3):
        for b in range(3):
            at = (2 - a) * cols
            total += dot(ds[2 - b, at : at + n, :], wd[3 * a + b], 1, 1)
    d = (total * slope(pre[...])).astype(BF16)
    fdelta[...] = d
    size = p0.shape[1]
    p2[...] = dot(d, block_of(w1, zone, 2, size), 1, 1).astype(BF16)
    p1[...] = dot(d, block_of(w1, zone, 1, size), 1, 1).astype(BF16)
    p3[...] = dot(d, block_of(w1, zone, 3, size), 1, 1).astype(BF16)
    p0[...] = dot(d, block_of(w1, zone, 0, size), 1, 1).astype(BF16)


def first_grad_kernel(zone_ref, own, left, right, far_a, far_b, delta, out):
    zone = zone_ref[0]
    half = far_a.shape[0]
    size = own.shape[1]
    d = delta[...]

    def put(step, v):
        which = lax.rem(zone + step, 4)
        out[pl.ds(pl.multiple_of(which * size, size), size), :] = v.astype(BF16)

    put(0, dot(own[...], d, 0, 0))
    put(3, dot(left[...], d, 0, 0))
    put(1, dot(right[...], d, 0, 0))
    put(2, dot(far_a[...], d[:half], 0, 0) + dot(far_b[...], d[half:], 0, 0))


def third_kernel(zone_ref, own, left, right, far_a, far_b, w3, grad, images, block_out, part):
    zone = zone_ref[0]
    half = far_a.shape[0]
    size = own.shape[1]
    for p, far in ((0, far_a), (1, far_b)):
        rows = pl.ds(p * half, half)
        v = dot(own[rows, :], block_of(w3, zone, 0, size))
        v += dot(left[rows, :], block_of(w3, zone, 3, size))
        v += dot(right[rows, :], block_of(w3, zone, 1, size))
        v += dot(far[...], block_of(w3, zone, 2, size))
        block_out[rows, :] = (images[rows, :].astype(F32) + v).astype(BF16)
    g = grad[...]

    def put(step, v):
        which = lax.rem(zone + step, 4)
        part[pl.ds(pl.multiple_of(which * size, size), size), :] = v.astype(BF16)

    put(0, dot(own[...], g, 0, 0))
    put(3, dot(left[...], g, 0, 0))
    put(1, dot(right[...], g, 0, 0))
    put(2, dot(far_a[...], g[:half], 0, 0) + dot(far_b[...], g[half:], 0, 0))


def body(images, first_weight, group_weight, third_weight, out_grad):
    rows_here, cols_all, chans_own = images.shape
    filt = lax.axis_size("filt")
    chan = lax.axis_size("chan")
    rows = lax.axis_size("rows")
    zones = filt // 2
    me = lax.axis_index("filt")
    core = lax.rem(me, 2)
    zone = (me // 2).astype(jnp.int32).reshape(1)
    cols = cols_all // 2
    pixels = rows_here * cols

    swap = [(i, i ^ 1) for i in range(filt)]
    zplus = [(z * 2 + c, (z + 1) % zones * 2 + c) for z in range(zones) for c in range(2)]
    zminus = [(t, s) for s, t in zplus]

    def halves(v, axis):
        n = v.shape[axis] // 2
        keep = lax.dynamic_slice_in_dim(v, core * n, n, axis)
        send = lax.dynamic_slice_in_dim(v, (1 - core) * n, n, axis)
        return keep, send

    def joined(keep, got, axis):
        return jnp.where(
            core == 0,
            jnp.concatenate([keep, got], axis),
            jnp.concatenate([got, keep], axis),
        )

    def core_swap(v):
        return lax.ppermute(v, "filt", swap)

    def split_pixels(v):
        keep, send = halves(v, 1)
        return joined(keep, core_swap(send), 2).reshape(pixels, 2 * chans_own)

    def merge_pixels(v):
        v = v.reshape(rows_here, cols, 2 * chans_own)
        keep, send = halves(v, 2)
        return joined(keep, core_swap(send), 1)

    def ring_gather(v):
        half = v.shape[0] // 2
        left = lax.ppermute(v, "filt", zplus)
        right = lax.ppermute(v, "filt", zminus)
        far_a = lax.ppermute(left[:half], "filt", zplus)
        far_b = lax.ppermute(right[half:], "filt", zminus)
        return v, left, right, far_a, far_b

    def ring_scatter(p1, p3, p2):
        half = p2.shape[0] // 2
        plus_b = lax.ppermute(p1[half:], "filt", zplus)
        got_a = lax.ppermute(p2[:half], "filt", zplus)
        minus_a = lax.ppermute(p3[:half], "filt", zminus)
        got_b = lax.ppermute(p2[half:], "filt", zminus)
        plus_a = lax.ppermute(
            (p1[:half].astype(F32) + got_a.astype(F32)).astype(BF16), "filt", zplus
        )
        minus_b = lax.ppermute(
            (p3[half:].astype(F32) + got_b.astype(F32)).astype(BF16), "filt", zminus
        )
        low = plus_a.astype(F32) + minus_a.astype(F32)
        high = plus_b.astype(F32) + minus_b.astype(F32)
        return jnp.concatenate([low, high], axis=0)

    col_next = [
        ((k * filt) + z * 2 + c, (k * filt + z * 2 + 1) if c == 0 else ((k + 1) * filt + z * 2))
        for k in range(chan)
        for z in range(zones)
        for c in range(2)
        if c == 0 or k < chan - 1
    ]
    col_prev = [(t, s) for s, t in col_next]
    row_next = [(i, i + 1) for i in range(rows - 1)]
    row_prev = [(t, s) for s, t in row_next]

    def halo(v):
        up = lax.ppermute(v[pixels - cols :], "rows", row_next)
        down = lax.ppermute(v[:cols], "rows", row_prev)
        own = v.reshape(rows_here, cols, v.shape[1])
        first = jnp.concatenate([up[:1], own[:, 0], down[:1]], axis=0)
        last = jnp.concatenate([up[cols - 1 :], own[:, cols - 1], down[cols - 1 :]], axis=0)
        low = lax.ppermute(last, ("chan", "filt"), col_next)
        high = lax.ppermute(first, ("chan", "filt"), col_prev)
        return up, v, down, low.astype(F32), high.astype(F32)

    def chan_gather(v):
        return lax.all_to_all(jnp.broadcast_to(v[None], (chan,) + v.shape), "chan", 0, 0)

    img = split_pixels(images)
    blocks = ring_gather(img)
    grad = split_pixels(out_grad)

    rows1, mid_own = first_weight.shape
    rows3, c_own = third_weight.shape
    wide = chan_gather(
        jnp.concatenate(
            [first_weight]
            + [third_weight[:, i : i + mid_own] for i in range(0, c_own, mid_own)],
            axis=0,
        )
    )
    wide_other = core_swap(wide)
    w1 = joined(wide[:, :rows1], wide_other[:, :rows1], 2).reshape(chan * rows1, 2 * mid_own)

    def third_of(w):
        return jnp.concatenate(
            [
                w[:, rows1 + i * rows3 : rows1 + (i + 1) * rows3]
                for i in range(c_own // mid_own)
            ],
            axis=2,
        )

    w3 = joined(third_of(wide), third_of(wide_other), 2).reshape(chan * rows3, 2 * c_own)

    size = group_weight.shape[2]
    taps = group_weight.reshape(9, size, mid_own)
    taps = joined(taps, core_swap(taps), 2)
    mid_here = 2 * mid_own
    diag = (jnp.arange(mid_here) // size)[:, None] == (jnp.arange(mid_here) // size)[None, :]
    wd = jnp.where(diag[None], jnp.tile(taps, (1, mid_here // size, 1)), 0).astype(BF16)

    m0, m1, m3, m2 = call(
        mid_kernel,
        [((pixels, mid_here), F32)] + [((pixels, mid_here), BF16)] * 3,
        1,
        (zone, grad, w3),
    )
    pre_first, act_first = call(
        first_kernel,
        [((pixels, mid_here), F32), ((pixels, mid_here), BF16)],
        1,
        (zone, *blocks, w1),
    )
    mid_rest = ring_scatter(m1, m3, m2)
    pre_group, act_group, xs = call(
        group_kernel,
        [
            ((pixels, mid_here), F32),
            ((pixels, mid_here), BF16),
            ((3, pixels + 2 * cols, mid_here), BF16),
        ],
        0,
        (*halo(act_first), wd),
    )
    delta = ((m0 + mid_rest) * slope(pre_group)).astype(BF16)
    delta_halo = halo(delta)
    acts = ring_gather(act_group)
    (group_part,) = call(group_grad_kernel, [((9, size, mid_here), F32)], 0, (xs, delta))

    first_delta, b0, b1, b3, b2 = call(
        back_kernel,
        [((pixels, mid_here), BF16)] + [((pixels, 2 * chans_own), BF16)] * 4,
        1,
        (zone, *delta_halo, wd, pre_first, w1),
        [pltpu.VMEM((3, pixels + 2 * cols, mid_here), BF16)],
    )
    back_rest = ring_scatter(b1, b3, b2)
    block_wide, third_part = call(
        third_kernel,
        [((pixels, 2 * chans_own), BF16), ((chan * rows3, 2 * c_own), BF16)],
        1,
        (zone, *acts, w3, grad, img),
    )
    block_out = merge_pixels(block_wide)
    (first_part,) = call(
        first_grad_kernel, [((chan * rows1, mid_here), BF16)], 1, (zone, *blocks, first_delta)
    )

    def over_cores(v, axis):
        keep, send = halves(v, axis)
        return (keep.astype(F32) + core_swap(send).astype(F32)).astype(BF16)

    third_half = over_cores(third_part, 1).reshape(chan, rows3, c_own)
    first_half = over_cores(first_part, 1).reshape(chan, rows1, mid_own)
    group_half = over_cores(group_part.astype(BF16), 2).reshape(9 * size, mid_own)
    packed = jnp.concatenate(
        [first_half]
        + [third_half[:, :, i : i + mid_own] for i in range(0, c_own, mid_own)]
        + [jnp.broadcast_to(group_half[None], (chan,) + group_half.shape)],
        axis=1,
    )
    packed = lax.all_to_all(packed, "chan", 0, 0)
    packed = jnp.sum(packed.astype(F32), axis=0).astype(BF16)
    ring = [(i, (i + 1) % rows) for i in range(rows)]
    back_ring = [(t, s) for s, t in ring]
    across = [(i, (i + 2) % rows) for i in range(rows)]
    before = lax.ppermute(packed, "rows", ring).astype(F32)
    after = lax.ppermute(packed, "rows", back_ring).astype(F32)
    opposite = lax.ppermute(packed, "rows", across).astype(F32)
    summed = (packed.astype(F32) + opposite) + (before + after)
    first_grad = summed[:rows1]
    third_grad = jnp.concatenate(
        [summed[rows1 + i * rows3 : rows1 + (i + 1) * rows3] for i in range(c_own // mid_own)],
        axis=1,
    )
    group_grad = summed[rows1 + rows3 * (c_own // mid_own) :].reshape(group_weight.shape)

    back = (b0.astype(F32) + back_rest).astype(BF16)
    images_grad = out_grad.astype(F32) + merge_pixels(back).astype(F32)
    return (block_out, images_grad, first_grad, group_grad, third_grad)


def solution(mesh):
    in_specs = (
        P("rows", "chan", "filt"),
        P("chan", "filt"),
        P(None, None, None, "filt"),
        P("chan", "filt"),
        P("rows", "chan", "filt"),
    )
    out_specs = (
        P("rows", "chan", "filt"),
        P("rows", "chan", "filt"),
        P("chan", "filt"),
        P(None, None, None, "filt"),
        P("chan", "filt"),
    )
    return jax.shard_map(body, mesh=mesh, in_specs=in_specs, out_specs=out_specs, check_vma=False)
```

```python
import jax
import jax.numpy as jnp
from jax import lax
from jax.experimental import pallas as pl
from jax.experimental.pallas import tpu as pltpu
from jax.sharding import PartitionSpec as P

F32 = jnp.float32
BF16 = jnp.bfloat16
VMEM = pl.BlockSpec(memory_space=pltpu.VMEM)
SMEM = pl.BlockSpec(memory_space=pltpu.SMEM)


def dot(a, b, ca=1, cb=0):
    return lax.dot_general(a, b, (((ca,), (cb,)), ((), ())), preferred_element_type=F32)


def call(kernel, outs, args, scratch=(), after=()):
    def ordered(*refs):
        kernel(*refs[: len(args)], *refs[len(args) + len(after) :])

    return pl.pallas_call(
        ordered,
        out_shape=[jax.ShapeDtypeStruct(s, d) for s, d in outs],
        in_specs=[SMEM]
        + [VMEM] * (len(args) - 1)
        + [pl.BlockSpec(memory_space=pl.ANY)] * len(after),
        out_specs=[VMEM] * len(outs),
        scratch_shapes=list(scratch),
        compiler_params=pltpu.CompilerParams(vmem_limit_bytes=48 * 2**20),
    )(*args, *after)


def span(index, size):
    return pl.ds(pl.multiple_of(index * size, size), size)


def logistic(v):
    return 1.0 / (1.0 + jnp.exp(-v))


def slope(v):
    s = logistic(v)
    return s * (1.0 + v * (1.0 - s))


def split_kernel(place, images, grad, own, send):
    core = lax.rem(place[0], 2)
    rows, cols = images.shape[0], images.shape[1] // 2
    for i, x in enumerate((images, grad)):
        for r in range(rows):
            at = slice(r * cols, (r + 1) * cols)
            own[i, at, :] = x[r, span(core, cols), :]
            send[i, at, :] = x[r, span(1 - core, cols), :]


def join_kernel(place, own, got, images, grad):
    for i, out in enumerate((images, grad)):
        out[0] = own[i]
        out[1] = got[i]


def gather_kernel(place, a0, a1, a2, a3, b0, b1, b2, b3, taps, taps_other, w1, w3, wd):
    core, chan = lax.rem(place[0], 2), place[2]
    low_z, y_here = lax.rem(chan, 2), chan // 2
    depth, half = w1.shape[1], a0.shape[2]
    mine, theirs = (a0, a1, a2, a3), (b0, b1, b2, b3)

    def fill(low, high, low_taps, high_taps):
        for step in range(4):
            y = y_here ^ step
            for s in range(2):
                k = 2 * y + (low_z ^ s)
                w1[k, :, :half] = low[step][s, :depth, :]
                w1[k, :, half:] = high[step][s, :depth, :]
                rows = span(low_z ^ s, half)
                for slot, refs in enumerate((mine, theirs)):
                    for i in range(2):
                        lanes = slice(i * half, (i + 1) * half)
                        at = slice(depth + i * half, depth + (i + 1) * half)
                        w3[y, slot, rows, lanes] = refs[step][s, at, :]
        chans = wd.shape[1]
        size = taps.shape[0] // 9
        row_group = lax.broadcasted_iota(jnp.int32, (chans, chans), 0) // size
        col_group = lax.broadcasted_iota(jnp.int32, (chans, chans), 1) // size
        keep = row_group == col_group
        both = jnp.concatenate([low_taps[...], high_taps[...]], axis=1).astype(F32)
        for t in range(9):
            whole = jnp.concatenate([both[t * size : (t + 1) * size]] * (chans // size), axis=0)
            wd[t] = jnp.where(keep, whole, 0.0).astype(BF16)

    @pl.when(core == 0)
    def _():
        fill(mine, theirs, taps, taps_other)

    @pl.when(core == 1)
    def _():
        fill(theirs, mine, taps_other, taps)


def block(place, step, slot):
    zone = lax.rem(place[0] // 2 + step, 4)
    return 2 * zone + (lax.rem(place[0], 2) ^ slot)


def outline(v, cols, top, bottom, first, last):
    rows = v.shape[0] // cols
    top[...] = v[:cols].astype(BF16)
    bottom[...] = v[(rows - 1) * cols :].astype(BF16)
    for out, c in ((first, 0), (last, cols - 1)):
        lines = [v[r * cols + c : r * cols + c + 1] for r in range(rows)]
        pad = jnp.zeros((out.shape[0] - rows - 1, v.shape[1]), F32)
        out[...] = jnp.concatenate([pad[:1]] + lines + [pad], axis=0).astype(BF16)


def first_kernel(place, own, left, right, far_a, far_b, w1, pre, act, top, bottom, first, last):
    total = None
    for step, slots in ((0, own), (3, left), (1, right), (2, (far_a, far_b))):
        for s in range(2):
            x = slots[s][...] if step == 2 else slots[s]
            v = dot(x, w1[block(place, step, s)])
            total = v if total is None else total + v
    pre[...] = total
    a = total * logistic(total)
    act[...] = a.astype(BF16)
    outline(a, top.shape[0], top, bottom, first, last)


def shifted(up, mid, down, low, high, out):
    cols, chans = up.shape
    n = mid.shape[0] + 2 * cols
    x = jnp.concatenate([up[...].astype(F32), mid[...].astype(F32), down[...].astype(F32)], axis=0)
    col = lax.rem(lax.broadcasted_iota(jnp.int32, (n, chans), 0), cols)

    def spread(edge):
        e = edge[...].astype(F32)
        parts = [jnp.broadcast_to(e[i : i + 1, :], (cols, chans)) for i in range(n // cols)]
        return jnp.concatenate(parts, axis=0)

    out[1] = x.astype(BF16)
    out[0] = jnp.where(col == 0, spread(low), pltpu.roll(x, 1, 0)).astype(BF16)
    out[2] = jnp.where(col == cols - 1, spread(high), pltpu.roll(x, n - 1, 0)).astype(BF16)


def group_kernel(place, up, mid, down, low, high, wd, pre, act, xs):
    n, cols = mid.shape[0], up.shape[0]
    shifted(up, mid, down, low, high, xs)
    total = None
    for a in range(3):
        for b in range(3):
            v = dot(xs[b, a * cols : a * cols + n, :], wd[3 * a + b])
            total = v if total is None else total + v
    pre[...] = total
    act[...] = (total * logistic(total)).astype(BF16)


def mid_kernel(place, grad, w3, p0, p1, p2a, p2b, p3):
    zone = place[0] // 2

    def part(step):
        z = lax.rem(zone + step, 4)
        return dot(grad[0], w3[z, 0], 1, 1) + dot(grad[1], w3[z, 1], 1, 1)

    half = p2a.shape[0]
    far = part(2).astype(BF16)
    p2a[...] = far[:half]
    p2b[...] = far[half:]
    p1[...] = part(1).astype(BF16)
    p3[...] = part(3).astype(BF16)
    p0[...] = part(0)


def pass_kernel(place, p1, p3, got_a, got_b, plus, minus):
    half = got_a.shape[0]
    plus[:half, :] = (p1[:half, :].astype(F32) + got_a[...].astype(F32)).astype(BF16)
    plus[half:, :] = p1[half:, :]
    minus[:half, :] = p3[:half, :]
    minus[half:, :] = (p3[half:, :].astype(F32) + got_b[...].astype(F32)).astype(BF16)


def delta_kernel(place, p0, plus, minus, pre, delta, top, bottom, first, last):
    mid = p0[...] + plus[...].astype(F32) + minus[...].astype(F32)
    d = mid * slope(pre[...])
    delta[...] = d.astype(BF16)
    outline(d, top.shape[0], top, bottom, first, last)


def back_kernel(place, up, mid, down, low, high, wd, pre, w1, fdelta, p0, p1, p2a, p2b, p3, ds):
    n, cols = mid.shape[0], up.shape[0]
    shifted(up, mid, down, low, high, ds)
    total = None
    for a in range(3):
        for b in range(3):
            at = (2 - a) * cols
            v = dot(ds[2 - b, at : at + n, :], wd[3 * a + b], 1, 1)
            total = v if total is None else total + v
    d = (total * slope(pre[...])).astype(BF16)
    fdelta[...] = d
    for s, out in ((0, p2a), (1, p2b)):
        out[...] = dot(d, w1[block(place, 2, s)], 1, 1).astype(BF16)
    for step, out in ((1, p1), (3, p3), (0, p0)):
        for s in range(2):
            v = dot(d, w1[block(place, step, s)], 1, 1)
            out[s * n : (s + 1) * n, :] = v.astype(out.dtype)


def combine_kernel(place, p0, plus, minus, keep, send):
    n = keep.shape[0]
    for s, out in ((0, keep), (1, send)):
        at = slice(s * n, (s + 1) * n)
        v = p0[at, :] + plus[at, :].astype(F32) + minus[at, :].astype(F32)
        out[...] = v.astype(out.dtype)


def merge_kernel(place, keep, got, out):
    core = lax.rem(place[0], 2)
    rows, cols = out.shape[0], out.shape[1] // 2
    for r in range(rows):
        at = slice(r * cols, (r + 1) * cols)
        out[r, span(core, cols), :] = keep[at, :]
        out[r, span(1 - core, cols), :] = got[at, :]


def merge_add_kernel(place, base, keep, got, out):
    core = lax.rem(place[0], 2)
    rows, cols = out.shape[0], out.shape[1] // 2
    for r in range(rows):
        at = slice(r * cols, (r + 1) * cols)
        for there, piece in ((span(core, cols), keep), (span(1 - core, cols), got)):
            out[r, there, :] = base[r, there, :].astype(F32) + piece[at, :].astype(F32)


def third_kernel(
    place, own, left, right, far_a, far_b, w3, grad, images, out_keep, out_send, keep, send
):
    zone = place[0] // 2
    acts = (
        (0, own[...]),
        (3, left[...]),
        (1, right[...]),
        (2, jnp.concatenate([far_a[...], far_b[...]], axis=0)),
    )
    for s, out in ((0, out_keep), (1, out_send)):
        total = images[s].astype(F32)
        third = None
        for step, a in acts:
            v = dot(a, w3[lax.rem(zone + step, 4), s])
            third = v if third is None else third + v
        out[...] = (total + third).astype(BF16)
    for step, a in acts:
        z = lax.rem(zone + step, 4)
        at = a.astype(F32).T.astype(BF16)
        size = at.shape[0]
        keep[span(z, size), :] = dot(at, grad[0])
        send[span(z, size), :] = dot(at, grad[1]).astype(BF16)


def group_grad_kernel(place, xs, delta, keep_out, send_out):
    core = lax.rem(place[0], 2)
    n, chans = delta.shape
    cols = (xs.shape[1] - n) // 2
    size = keep_out.shape[0] * 2 // 9
    wide = chans // 2
    d = delta[...]
    row_group = lax.broadcasted_iota(jnp.int32, (chans, chans), 0) // size
    col_group = lax.broadcasted_iota(jnp.int32, (chans, chans), 1) // size
    diag = row_group == col_group
    taps = []
    for t in range(9):
        a, b = t // 3, t % 3
        full = jnp.where(diag, dot(xs[b, a * cols : a * cols + n, :], d, 0, 0), 0.0)
        total = full[0:size]
        for g in range(1, chans // size):
            total += full[g * size : (g + 1) * size]
        taps.append(total)
    both = jnp.concatenate(taps, axis=0)
    half = both.shape[0] // 2
    low = jnp.concatenate([both[:half, :wide], both[half:, :wide]], axis=1)
    high = jnp.concatenate([both[:half, wide:], both[half:, wide:]], axis=1)
    keep_out[...] = jnp.where(core == 0, low, high)
    send_out[...] = jnp.where(core == 0, high, low).astype(BF16)


def first_grad_kernel(
    place, own, left, right, far_a, far_b, delta, group_keep, group_send, keep, send
):
    core = lax.rem(place[0], 2)
    d = delta[...].astype(F32).T.astype(BF16)
    rows = d.shape[0] // 2
    for step, slots in ((0, own), (3, left), (1, right), (2, (far_a, far_b))):
        for s in range(2):
            v = dot(d, slots[s][...] if step == 2 else slots[s])
            low, high = v[:rows], v[rows:]
            at = span(block(place, step, s), rows)
            keep[at, :] = jnp.where(core == 0, low, high)
            send[at, :] = jnp.where(core == 0, high, low).astype(BF16)
    keep[8 * rows :, :] = group_keep[...]
    send[8 * rows :, :] = group_send[...]


def pack_kernel(place, keep, got, third_keep, third_got, o0, o1, o2, o3):
    low_z, y_here = lax.rem(place[2], 2), place[2] // 2
    rows = third_keep.shape[0] // 8
    group = keep.shape[0] - 8 * rows
    part = (keep[8 * rows :, :] + got[8 * rows :, :].astype(F32)).astype(BF16)
    for step, out in enumerate((o0, o1, o2, o3)):
        for s in range(2):
            at = span(2 * (y_here ^ step) + (low_z ^ s), rows)
            out[s, :rows, :] = (keep[at, :] + got[at, :].astype(F32)).astype(BF16)
            out[s, rows : rows + group, :] = part
            v = third_keep[at, :] + third_got[at, :].astype(F32)
            out[s, rows + group :, :] = v.astype(BF16)


def sum_kernel(place, a, b, c, d, keep, send):
    for s, out in ((0, keep), (1, send)):
        v = (a[s].astype(F32) + c[s].astype(F32)) + (b[s].astype(F32) + d[s].astype(F32))
        out[...] = v.astype(out.dtype)


def add_kernel(place, keep, got, out):
    out[...] = (keep[...] + got[...].astype(F32)).astype(BF16)


def last_kernel(place, own, a, b, c, first, group, third):
    total = (own[...].astype(F32) + b[...].astype(F32)) + (
        a[...].astype(F32) + c[...].astype(F32)
    )
    wide = first.shape[1]
    half = group.shape[0] // 2
    first[...] = total[:wide].T
    group[:half, :] = total[wide : wide + half, :wide]
    group[half:, :] = total[wide : wide + half, wide:]
    third[...] = total[wide + half :]


def body(images, first_weight, group_weight, third_weight, out_grad):
    rows_here, cols_here, chans = images.shape
    filt, chan, rows = lax.axis_size("filt"), lax.axis_size("chan"), lax.axis_size("rows")
    zones = filt // 2
    place = jnp.stack([lax.axis_index(a) for a in ("filt", "rows", "chan")]).astype(jnp.int32)
    cols = cols_here // 2
    n = rows_here * cols
    depth, own_mid = first_weight.shape
    hidden = 2 * own_mid
    pair = (2, n, chans)

    def xor(axis, k):
        return [(i, i ^ k) for i in range(lax.axis_size(axis))]

    zplus = [(z * 2 + c, (z + 1) % zones * 2 + c) for z in range(zones) for c in range(2)]
    zminus = [(t, s) for s, t in zplus]
    row_next = [(i, i + 1) for i in range(rows - 1)]
    row_prev = [(t, s) for s, t in row_next]
    col_next = [
        (k * filt + 2 * z + c, k * filt + 2 * z + 1 if c == 0 else (k + 1) * filt + 2 * z)
        for k in range(chan)
        for z in range(zones)
        for c in range(2)
        if c == 0 or k < chan - 1
    ]
    col_prev = [(t, s) for s, t in col_next]

    def swap(v):
        return lax.ppermute(v, "filt", xor("filt", 1))

    def up_z(v):
        return lax.ppermute(v, "filt", zplus)

    def down_z(v):
        return lax.ppermute(v, "filt", zminus)

    def along_y(pieces):
        return [pieces[0]] + [
            lax.ppermute(pieces[k], "chan", xor("chan", 2 * k)) for k in range(1, 4)
        ]

    def ring_scatter(p0, p1, p2a, p2b, p3, after=()):
        shape = p1.shape
        plus, minus = call(
            pass_kernel,
            [(shape, BF16)] * 2,
            (place, p1, p3, up_z(p2a), down_z(p2b)),
            after=after,
        )
        return (p0, up_z(plus), down_z(minus)), plus

    def halo(v, top, bottom, first, last):
        up = lax.ppermute(bottom, "rows", row_next)
        down = lax.ppermute(top, "rows", row_prev)

        def line(edge, c):
            end = slice(c, c + 1)
            return jnp.concatenate(
                [up[end], edge[1 : rows_here + 1], down[end], edge[rows_here + 2 :]], axis=0
            )

        low = lax.ppermute(line(last, cols - 1), ("chan", "filt"), col_next)
        high = lax.ppermute(line(first, 0), ("chan", "filt"), col_prev)
        return up, v, down, low, high

    panel = jnp.concatenate(
        [first_weight] + [third_weight[:, i : i + own_mid] for i in range(0, chans, own_mid)],
        axis=0,
    )
    taps = group_weight.reshape(-1, own_mid)
    beside = lax.ppermute(panel, "chan", xor("chan", 1))

    own, send = call(split_kernel, [(pair, BF16)] * 2, (place, images, out_grad))
    img, grad = call(
        join_kernel, [(pair, BF16)] * 2, (place, own, swap(send)), after=(beside,)
    )
    left, right = up_z(img), down_z(img)
    blocks = (img, left, right, up_z(left[0]), down_z(right[1]))

    panel = jnp.stack([panel, beside])
    panels = along_y([panel] * 4)
    w1, w3, wd = call(
        gather_kernel,
        [
            ((chan, depth, hidden), BF16),
            ((zones, 2, hidden, chans), BF16),
            ((9, hidden, hidden), BF16),
        ],
        (place, *panels, *[swap(p) for p in panels], taps, swap(taps)),
    )

    flat = (n, hidden)
    half = (n // 2, hidden)
    mid_parts = call(
        mid_kernel,
        [(flat, F32), (flat, BF16), (half, BF16), (half, BF16), (flat, BF16)],
        (place, grad, w3),
    )
    mid_parts, passed = ring_scatter(*mid_parts)
    around = [((cols, hidden), BF16)] * 2 + [((16, hidden), BF16)] * 2
    pre_first, act_first, *edge = call(
        first_kernel,
        [(flat, F32), (flat, BF16)] + around,
        (place, *blocks, w1),
        after=(passed,),
    )
    pre_group, act_group, xs = call(
        group_kernel,
        [(flat, F32), (flat, BF16), ((3, n + 2 * cols, hidden), BF16)],
        (place, *halo(act_first, *edge), wd),
    )
    act_left, act_right = up_z(act_group), down_z(act_group)
    delta, *edge = call(
        delta_kernel, [(flat, BF16)] + around, (place, *mid_parts, pre_group)
    )
    acts = (
        act_group,
        act_left,
        act_right,
        up_z(act_left[: n // 2]),
        down_z(act_right[n // 2 :]),
    )
    two = (2 * n, chans)
    first_delta, *back_parts = call(
        back_kernel,
        [(flat, BF16), (two, F32), (two, BF16)] + [((n, chans), BF16)] * 2 + [(two, BF16)],
        (place, *halo(delta, *edge), wd, pre_first, w1),
        [pltpu.VMEM((3, n + 2 * cols, hidden), BF16)],
        after=(act_left, act_right),
    )
    group_keep, group_send = call(
        group_grad_kernel,
        [((taps.shape[0] // 2, hidden), F32), ((taps.shape[0] // 2, hidden), BF16)],
        (place, xs, delta),
    )

    out_keep, out_send, third_keep, third_send = call(
        third_kernel,
        [((n, chans), BF16)] * 2
        + [((chan * own_mid, chans), F32), ((chan * own_mid, chans), BF16)],
        (place, *acts, w3, grad, img),
        after=(first_delta,),
    )
    (block_out,) = call(
        merge_kernel, [(images.shape, BF16)], (place, out_keep, swap(out_send))
    )

    lines = own_mid + taps.shape[0] // 2
    keep, send = call(
        first_grad_kernel,
        [((lines + (chan - 1) * own_mid, chans), d) for d in (F32, BF16)],
        (place, *blocks, first_delta, group_keep, group_send),
    )
    back_parts, passed = ring_scatter(*back_parts, after=(keep, third_keep))
    lines += own_mid
    pieces = call(
        pack_kernel,
        [((2, lines, chans), BF16)] * 4,
        (place, keep, swap(send), third_keep, swap(third_send)),
    )
    keep, send = call(
        sum_kernel,
        [((lines, chans), F32), ((lines, chans), BF16)],
        (place, *along_y(pieces)),
    )
    (total,) = call(
        add_kernel,
        [((lines, chans), BF16)],
        (place, keep, lax.ppermute(send, "chan", xor("chan", 1))),
    )
    others = [lax.ppermute(total, "rows", xor("rows", k)) for k in range(1, 4)]
    first_grad, group_grad, third_grad = call(
        last_kernel,
        [((depth, own_mid), F32), (taps.shape, F32), ((own_mid, chans), F32)],
        (place, total, *others),
    )

    keep, send = call(
        combine_kernel, [((n, chans), F32), ((n, chans), BF16)], (place, *back_parts)
    )
    (images_grad,) = call(
        merge_add_kernel, [(images.shape, F32)], (place, out_grad, keep, swap(send))
    )
    return (block_out, images_grad, first_grad, group_grad.reshape(group_weight.shape), third_grad)


def solution(mesh):
    in_specs = (
        P("rows", "chan", "filt"),
        P("chan", "filt"),
        P(None, None, None, "filt"),
        P("chan", "filt"),
        P("rows", "chan", "filt"),
    )
    out_specs = (
        P("rows", "chan", "filt"),
        P("rows", "chan", "filt"),
        P("chan", "filt"),
        P(None, None, None, "filt"),
        P("chan", "filt"),
    )
    return jax.shard_map(body, mesh=mesh, in_specs=in_specs, out_specs=out_specs, check_vma=False)
```

```python
import jax
import jax.numpy as jnp
from jax import lax
from jax.experimental import pallas as pl
from jax.experimental.pallas import tpu as pltpu
from jax.sharding import PartitionSpec as P

F32 = jnp.float32
BF16 = jnp.bfloat16
VMEM = pl.BlockSpec(memory_space=pltpu.VMEM)
SMEM = pl.BlockSpec(memory_space=pltpu.SMEM)


def dot(a, b, ca=1, cb=0):
    return lax.dot_general(a, b, (((ca,), (cb,)), ((), ())), preferred_element_type=F32)


def call(kernel, outs, args, scratch=(), after=()):
    def ordered(*refs):
        kernel(*refs[: len(args)], *refs[len(args) + len(after) :])

    weight = WEIGHT.get(kernel.__name__, 1)
    with jax.named_scope(kernel.__name__):
        return pl.pallas_call(
            ordered,
            out_shape=[jax.ShapeDtypeStruct(s, d) for s, d in outs],
            in_specs=[SMEM]
            + [VMEM] * (len(args) - 1)
            + [pl.BlockSpec(memory_space=pl.ANY)] * len(after),
            out_specs=[VMEM] * len(outs),
            scratch_shapes=list(scratch),
            cost_estimate=pl.CostEstimate(flops=weight, bytes_accessed=weight, transcendentals=0),
            compiler_params=pltpu.CompilerParams(vmem_limit_bytes=48 * 2**20),
        )(*args, *after)


WEIGHT = {"back_kernel": 3 * 10**10}


def span(index, size):
    return pl.ds(pl.multiple_of(index * size, size), size)


def logistic(v):
    return 1.0 / (1.0 + jnp.exp(-v))


def slope(v):
    s = logistic(v)
    return s * (1.0 + v * (1.0 - s))


def split_kernel(place, images, grad, own, send):
    core = lax.rem(place[0], 2)
    rows, cols = images.shape[0], images.shape[1] // 2
    for i, x in enumerate((images, grad)):
        for r in range(rows):
            at = slice(r * cols, (r + 1) * cols)
            own[i, at, :] = x[r, span(core, cols), :]
            send[i, at, :] = x[r, span(1 - core, cols), :]


def join_kernel(place, own, got, images, grad):
    for i, out in enumerate((images, grad)):
        out[0] = own[i]
        out[1] = got[i]


def panel_kernel(place, first, third, first_got, third_got, out):
    depth, wide = first.shape
    for s, (a, b) in enumerate(((first, third), (first_got, third_got))):
        out[s, :depth, :] = a[...]
        for i in range(b.shape[1] // wide):
            at = slice(depth + i * b.shape[0], depth + (i + 1) * b.shape[0])
            out[s, at, :] = b[:, i * wide : (i + 1) * wide]


def gather_kernel(place, a0, a1, a2, a3, b0, b1, b2, b3, taps, taps_other, w1, w3, wd):
    core, chan = lax.rem(place[0], 2), place[2]
    low_z, y_here = lax.rem(chan, 2), chan // 2
    depth, half = w1.shape[1], a0.shape[2]
    mine, theirs = (a0, a1, a2, a3), (b0, b1, b2, b3)

    def fill(low, high, low_taps, high_taps):
        for step in range(4):
            y = y_here ^ step
            for s in range(2):
                k = 2 * y + (low_z ^ s)
                w1[k, :, :half] = low[step][s, :depth, :]
                w1[k, :, half:] = high[step][s, :depth, :]
                rows = span(low_z ^ s, half)
                for slot, refs in enumerate((mine, theirs)):
                    for i in range(2):
                        lanes = slice(i * half, (i + 1) * half)
                        at = slice(depth + i * half, depth + (i + 1) * half)
                        w3[y, slot, rows, lanes] = refs[step][s, at, :]
        chans = wd.shape[1]
        size = taps.shape[0] // 9
        row_group = lax.broadcasted_iota(jnp.int32, (chans, chans), 0) // size
        col_group = lax.broadcasted_iota(jnp.int32, (chans, chans), 1) // size
        keep = row_group == col_group
        both = jnp.concatenate([low_taps[...], high_taps[...]], axis=1).astype(F32)
        for t in range(9):
            whole = jnp.concatenate([both[t * size : (t + 1) * size]] * (chans // size), axis=0)
            wd[t] = jnp.where(keep, whole, 0.0).astype(BF16)

    @pl.when(core == 0)
    def _():
        fill(mine, theirs, taps, taps_other)

    @pl.when(core == 1)
    def _():
        fill(theirs, mine, taps_other, taps)


def block(place, step, slot):
    zone = lax.rem(place[0] // 2 + step, 4)
    return 2 * zone + (lax.rem(place[0], 2) ^ slot)


def outline(v, cols, top, bottom, first, last):
    rows = v.shape[0] // cols
    top[...] = v[:cols].astype(BF16)
    bottom[...] = v[(rows - 1) * cols :].astype(BF16)
    for out, c in ((first, 0), (last, cols - 1)):
        lines = [v[r * cols + c : r * cols + c + 1] for r in range(rows)]
        pad = jnp.zeros((out.shape[0] - rows - 1, v.shape[1]), F32)
        out[...] = jnp.concatenate([pad[:1]] + lines + [pad], axis=0).astype(BF16)


def first_kernel(place, own, left, right, far_a, far_b, w1, pre, act, top, bottom, first, last):
    total = None
    for step, slots in ((0, own), (3, left), (1, right), (2, (far_a, far_b))):
        for s in range(2):
            x = slots[s][...] if step == 2 else slots[s]
            v = dot(x, w1[block(place, step, s)])
            total = v if total is None else total + v
    pre[...] = total
    a = total * logistic(total)
    act[...] = a.astype(BF16)
    outline(a, top.shape[0], top, bottom, first, last)


def shifted(up, mid, down, low, high, out):
    cols, chans = up.shape
    n = mid.shape[0] + 2 * cols
    x = jnp.concatenate([up[...].astype(F32), mid[...].astype(F32), down[...].astype(F32)], axis=0)
    col = lax.rem(lax.broadcasted_iota(jnp.int32, (n, chans), 0), cols)

    def spread(edge):
        e = edge[...].astype(F32)
        parts = [jnp.broadcast_to(e[i : i + 1, :], (cols, chans)) for i in range(n // cols)]
        return jnp.concatenate(parts, axis=0)

    out[1] = x.astype(BF16)
    out[0] = jnp.where(col == 0, spread(low), pltpu.roll(x, 1, 0)).astype(BF16)
    out[2] = jnp.where(col == cols - 1, spread(high), pltpu.roll(x, n - 1, 0)).astype(BF16)


def group_kernel(place, up, mid, down, low, high, wd, pre, act, xs):
    n, cols = mid.shape[0], up.shape[0]
    shifted(up, mid, down, low, high, xs)
    total = None
    for a in range(3):
        for b in range(3):
            v = dot(xs[b, a * cols : a * cols + n, :], wd[3 * a + b])
            total = v if total is None else total + v
    pre[...] = total
    act[...] = (total * logistic(total)).astype(BF16)


def mid_kernel(place, grad, w3, p0, p1, p2a, p2b, p3):
    zone = place[0] // 2

    def part(step):
        z = lax.rem(zone + step, 4)
        return dot(grad[0], w3[z, 0], 1, 1) + dot(grad[1], w3[z, 1], 1, 1)

    half = p2a.shape[0]
    far = part(2).astype(BF16)
    p2a[...] = far[:half]
    p2b[...] = far[half:]
    p1[...] = part(1).astype(BF16)
    p3[...] = part(3).astype(BF16)
    p0[...] = part(0)


def pass_kernel(place, p1, p3, got_a, got_b, plus, minus):
    half = got_a.shape[0]
    plus[:half, :] = (p1[:half, :].astype(F32) + got_a[...].astype(F32)).astype(BF16)
    plus[half:, :] = p1[half:, :]
    minus[:half, :] = p3[:half, :]
    minus[half:, :] = (p3[half:, :].astype(F32) + got_b[...].astype(F32)).astype(BF16)


def delta_kernel(place, p0, plus, minus, pre, delta, top, bottom, first, last):
    mid = p0[...] + plus[...].astype(F32) + minus[...].astype(F32)
    d = mid * slope(pre[...])
    delta[...] = d.astype(BF16)
    outline(d, top.shape[0], top, bottom, first, last)


def back_kernel(place, up, mid, down, low, high, wd, pre, w1, fdelta, p0, p1, p2a, p2b, p3, ds):
    n, cols = mid.shape[0], up.shape[0]
    shifted(up, mid, down, low, high, ds)
    total = None
    for a in range(3):
        for b in range(3):
            at = (2 - a) * cols
            v = dot(ds[2 - b, at : at + n, :], wd[3 * a + b], 1, 1)
            total = v if total is None else total + v
    d = (total * slope(pre[...])).astype(BF16)
    fdelta[...] = d
    for s, out in ((0, p2a), (1, p2b)):
        out[...] = dot(d, w1[block(place, 2, s)], 1, 1).astype(BF16)
    for step, out in ((1, p1), (3, p3), (0, p0)):
        for s in range(2):
            v = dot(d, w1[block(place, step, s)], 1, 1)
            out[s * n : (s + 1) * n, :] = v.astype(out.dtype)


def combine_kernel(place, p0, plus, minus, keep, send):
    n = keep.shape[0]
    for s, out in ((0, keep), (1, send)):
        at = slice(s * n, (s + 1) * n)
        v = p0[at, :] + plus[at, :].astype(F32) + minus[at, :].astype(F32)
        out[...] = v.astype(out.dtype)


def merge_kernel(place, keep, got, out):
    core = lax.rem(place[0], 2)
    rows, cols = out.shape[0], out.shape[1] // 2
    for r in range(rows):
        at = slice(r * cols, (r + 1) * cols)
        out[r, span(core, cols), :] = keep[at, :]
        out[r, span(1 - core, cols), :] = got[at, :]


def merge_add_kernel(place, base, keep, got, out):
    core = lax.rem(place[0], 2)
    rows, cols = out.shape[0], out.shape[1] // 2
    for r in range(rows):
        at = slice(r * cols, (r + 1) * cols)
        for there, piece in ((span(core, cols), keep), (span(1 - core, cols), got)):
            out[r, there, :] = base[r, there, :].astype(F32) + piece[at, :].astype(F32)


def third_kernel(
    place, own, left, right, far_a, far_b, w3, grad, images, out_keep, out_send, keep, send
):
    zone = place[0] // 2
    acts = (
        (0, own[...]),
        (3, left[...]),
        (1, right[...]),
        (2, jnp.concatenate([far_a[...], far_b[...]], axis=0)),
    )
    for s, out in ((0, out_keep), (1, out_send)):
        total = images[s].astype(F32)
        third = None
        for step, a in acts:
            v = dot(a, w3[lax.rem(zone + step, 4), s])
            third = v if third is None else third + v
        out[...] = (total + third).astype(BF16)
    for step, a in acts:
        z = lax.rem(zone + step, 4)
        at = a.astype(F32).T.astype(BF16)
        size = at.shape[0]
        keep[span(z, size), :] = dot(at, grad[0])
        send[span(z, size), :] = dot(at, grad[1]).astype(BF16)


def group_grad_kernel(place, xs, delta, keep_out, send_out):
    core = lax.rem(place[0], 2)
    n, chans = delta.shape
    cols = (xs.shape[1] - n) // 2
    size = keep_out.shape[0] * 2 // 9
    wide = chans // 2
    d = delta[...]
    row_group = lax.broadcasted_iota(jnp.int32, (chans, chans), 0) // size
    col_group = lax.broadcasted_iota(jnp.int32, (chans, chans), 1) // size
    diag = row_group == col_group
    taps = []
    for t in range(9):
        a, b = t // 3, t % 3
        full = jnp.where(diag, dot(xs[b, a * cols : a * cols + n, :], d, 0, 0), 0.0)
        total = full[0:size]
        for g in range(1, chans // size):
            total += full[g * size : (g + 1) * size]
        taps.append(total)
    both = jnp.concatenate(taps, axis=0)
    half = both.shape[0] // 2
    low = jnp.concatenate([both[:half, :wide], both[half:, :wide]], axis=1)
    high = jnp.concatenate([both[:half, wide:], both[half:, wide:]], axis=1)
    keep_out[...] = jnp.where(core == 0, low, high)
    send_out[...] = jnp.where(core == 0, high, low).astype(BF16)


def first_grad_kernel(
    place, own, left, right, far_a, far_b, delta, group_keep, group_send, keep, send
):
    core = lax.rem(place[0], 2)
    d = delta[...].astype(F32).T.astype(BF16)
    rows = d.shape[0] // 2
    for step, slots in ((0, own), (3, left), (1, right), (2, (far_a, far_b))):
        for s in range(2):
            v = dot(d, slots[s][...] if step == 2 else slots[s])
            low, high = v[:rows], v[rows:]
            at = span(block(place, step, s), rows)
            keep[at, :] = jnp.where(core == 0, low, high)
            send[at, :] = jnp.where(core == 0, high, low).astype(BF16)
    keep[8 * rows :, :] = group_keep[...]
    send[8 * rows :, :] = group_send[...]


def pack_kernel(place, keep, got, third_keep, third_got, o0, o1, o2, o3):
    low_z, y_here = lax.rem(place[2], 2), place[2] // 2
    rows = third_keep.shape[0] // 8
    part = (keep[8 * rows :, :] + got[8 * rows :, :].astype(F32)).astype(BF16)
    for step, out in enumerate((o0, o1, o2, o3)):
        for s in range(2):
            at = span(2 * (y_here ^ step) + (low_z ^ s), rows)
            v = keep[at, :] + got[at, :].astype(F32)
            out[2 * s * rows : (2 * s + 1) * rows, :] = v.astype(BF16)
            v = third_keep[at, :] + third_got[at, :].astype(F32)
            out[(2 * s + 1) * rows : (2 * s + 2) * rows, :] = v.astype(BF16)
        out[4 * rows :, :] = part


def sum_y_kernel(place, a, b, c, d, out):
    v = (a[...].astype(F32) + c[...].astype(F32)) + (b[...].astype(F32) + d[...].astype(F32))
    out[...] = v.astype(BF16)


def sum_kernel(place, a, b, c, d, keep, send):
    v = (a[...].astype(F32) + c[...].astype(F32)) + (b[...].astype(F32) + d[...].astype(F32))
    keep[...] = v[: keep.shape[0]]
    send[...] = v[keep.shape[0] :].astype(BF16)


def last_kernel(place, keep, send, got, first, group, third):
    mine = keep.shape[0]
    wide = first.shape[1]
    total = keep[...] + got[:mine, :].astype(F32)
    first[...] = total[:wide].T
    third[...] = total[wide:]
    part = send[mine:, :].astype(F32) + got[mine:, :].astype(F32)
    half = group.shape[0] // 2
    group[:half, :] = part[:, :wide]
    group[half:, :] = part[:, wide:]


def body(images, first_weight, group_weight, third_weight, out_grad):
    rows_here, cols_here, chans = images.shape
    filt, chan, rows = lax.axis_size("filt"), lax.axis_size("chan"), lax.axis_size("rows")
    zones = filt // 2
    place = jnp.stack([lax.axis_index(a) for a in ("filt", "rows", "chan")]).astype(jnp.int32)
    cols = cols_here // 2
    n = rows_here * cols
    depth, own_mid = first_weight.shape
    hidden = 2 * own_mid
    pair = (2, n, chans)

    def xor(axis, k):
        return [(i, i ^ k) for i in range(lax.axis_size(axis))]

    zplus = [(z * 2 + c, (z + 1) % zones * 2 + c) for z in range(zones) for c in range(2)]
    zminus = [(t, s) for s, t in zplus]
    row_next = [(i, i + 1) for i in range(rows - 1)]
    row_prev = [(t, s) for s, t in row_next]
    col_next = [
        (k * filt + 2 * z + c, k * filt + 2 * z + 1 if c == 0 else (k + 1) * filt + 2 * z)
        for k in range(chan)
        for z in range(zones)
        for c in range(2)
        if c == 0 or k < chan - 1
    ]
    col_prev = [(t, s) for s, t in col_next]

    def swap(v):
        return lax.ppermute(v, "filt", xor("filt", 1))

    def up_z(v):
        return lax.ppermute(v, "filt", zplus)

    def down_z(v):
        return lax.ppermute(v, "filt", zminus)

    def along_y(pieces):
        return [pieces[0]] + [
            lax.ppermute(pieces[k], "chan", xor("chan", 2 * k)) for k in range(1, 4)
        ]

    def ring_scatter(p0, p1, p2a, p2b, p3, after=()):
        shape = p1.shape
        plus, minus = call(
            pass_kernel,
            [(shape, BF16)] * 2,
            (place, p1, p3, up_z(p2a), down_z(p2b)),
            after=after,
        )
        return (p0, up_z(plus), down_z(minus)), plus

    def halo(v, top, bottom, first, last):
        up = lax.ppermute(bottom, "rows", row_next)
        down = lax.ppermute(top, "rows", row_prev)

        def line(edge, c):
            end = slice(c, c + 1)
            return jnp.concatenate(
                [up[end], edge[1 : rows_here + 1], down[end], edge[rows_here + 2 :]], axis=0
            )

        low = lax.ppermute(line(last, cols - 1), ("chan", "filt"), col_next)
        high = lax.ppermute(line(first, 0), ("chan", "filt"), col_prev)
        return up, v, down, low, high

    taps = group_weight.reshape(-1, own_mid)
    beside = [lax.ppermute(w, "chan", xor("chan", 1)) for w in (first_weight, third_weight)]

    own, send = call(split_kernel, [(pair, BF16)] * 2, (place, images, out_grad))
    img, grad = call(
        join_kernel, [(pair, BF16)] * 2, (place, own, swap(send)), after=beside
    )
    left, right = up_z(img), down_z(img)
    blocks = (img, left, right, up_z(left[0]), down_z(right[1]))

    (panel,) = call(
        panel_kernel,
        [((2, depth + third_weight.size // own_mid, own_mid), BF16)],
        (place, first_weight, third_weight, *beside),
        after=(img,),
    )
    panels = along_y([panel] * 4)
    w1, w3, wd = call(
        gather_kernel,
        [
            ((chan, depth, hidden), BF16),
            ((zones, 2, hidden, chans), BF16),
            ((9, hidden, hidden), BF16),
        ],
        (place, *panels, *[swap(p) for p in panels], taps, swap(taps)),
    )

    flat = (n, hidden)
    half = (n // 2, hidden)
    mid_parts = call(
        mid_kernel,
        [(flat, F32), (flat, BF16), (half, BF16), (half, BF16), (flat, BF16)],
        (place, grad, w3),
    )
    mid_parts, passed = ring_scatter(*mid_parts)
    around = [((cols, hidden), BF16)] * 2 + [((16, hidden), BF16)] * 2
    pre_first, act_first, *edge = call(
        first_kernel,
        [(flat, F32), (flat, BF16)] + around,
        (place, *blocks, w1),
    )
    pre_group, act_group, xs = call(
        group_kernel,
        [(flat, F32), (flat, BF16), ((3, n + 2 * cols, hidden), BF16)],
        (place, *halo(act_first, *edge), wd),
        after=(passed,),
    )
    act_left, act_right = up_z(act_group), down_z(act_group)
    delta, *edge = call(
        delta_kernel, [(flat, BF16)] + around, (place, *mid_parts, pre_group)
    )
    acts = (
        act_group,
        act_left,
        act_right,
        up_z(act_left[: n // 2]),
        down_z(act_right[n // 2 :]),
    )
    two = (2 * n, chans)
    first_delta, *back_parts = call(
        back_kernel,
        [(flat, BF16), (two, F32), (two, BF16)] + [((n, chans), BF16)] * 2 + [(two, BF16)],
        (place, *halo(delta, *edge), wd, pre_first, w1),
        [pltpu.VMEM((3, n + 2 * cols, hidden), BF16)],
        after=(act_left, act_right),
    )
    group_keep, group_send = call(
        group_grad_kernel,
        [((taps.shape[0] // 2, hidden), F32), ((taps.shape[0] // 2, hidden), BF16)],
        (place, xs, delta),
    )

    out_keep, out_send, third_keep, third_send = call(
        third_kernel,
        [((n, chans), BF16)] * 2
        + [((chan * own_mid, chans), F32), ((chan * own_mid, chans), BF16)],
        (place, *acts, w3, grad, img),
        after=(first_delta,),
    )
    (block_out,) = call(
        merge_kernel, [(images.shape, BF16)], (place, out_keep, swap(out_send))
    )

    lines = own_mid + taps.shape[0] // 2
    keep, send = call(
        first_grad_kernel,
        [((lines + (chan - 1) * own_mid, chans), d) for d in (F32, BF16)],
        (place, *blocks, first_delta, group_keep, group_send),
    )
    back_parts, passed = ring_scatter(*back_parts, after=(keep, third_keep))
    lines += own_mid
    pieces = call(
        pack_kernel,
        [((lines + 2 * own_mid, chans), BF16)] * 4,
        (place, keep, swap(send), third_keep, swap(third_send)),
    )
    lined = [((lines + 2 * own_mid, chans), BF16)]
    (total,) = call(sum_y_kernel, lined, (place, *along_y(pieces)))
    others = [lax.ppermute(total, "rows", xor("rows", k)) for k in range(1, 4)]
    keep, send = call(
        sum_kernel,
        [((2 * own_mid, chans), F32), ((lines, chans), BF16)],
        (place, total, *others),
    )
    first_grad, group_grad, third_grad = call(
        last_kernel,
        [((depth, own_mid), F32), (taps.shape, F32), ((own_mid, chans), F32)],
        (place, keep, send, lax.ppermute(send, "chan", xor("chan", 1))),
    )

    keep, send = call(
        combine_kernel, [((n, chans), F32), ((n, chans), BF16)], (place, *back_parts)
    )
    (images_grad,) = call(
        merge_add_kernel, [(images.shape, F32)], (place, out_grad, keep, swap(send))
    )
    return (block_out, images_grad, first_grad, group_grad.reshape(group_weight.shape), third_grad)


def solution(mesh):
    in_specs = (
        P("rows", "chan", "filt"),
        P("chan", "filt"),
        P(None, None, None, "filt"),
        P("chan", "filt"),
        P("rows", "chan", "filt"),
    )
    out_specs = (
        P("rows", "chan", "filt"),
        P("rows", "chan", "filt"),
        P("chan", "filt"),
        P(None, None, None, "filt"),
        P("chan", "filt"),
    )
    return jax.shard_map(body, mesh=mesh, in_specs=in_specs, out_specs=out_specs, check_vma=False)
```

```python
import jax
import jax.numpy as jnp
from jax import lax
from jax.experimental import pallas as pl
from jax.experimental.pallas import tpu as pltpu
from jax.sharding import PartitionSpec as P

F32 = jnp.float32
BF16 = jnp.bfloat16
VMEM = pl.BlockSpec(memory_space=pltpu.VMEM)
SMEM = pl.BlockSpec(memory_space=pltpu.SMEM)


def dot(a, b, ca=1, cb=0):
    return lax.dot_general(a, b, (((ca,), (cb,)), ((), ())), preferred_element_type=F32)


def call(kernel, outs, args, scratch=(), after=()):
    def ordered(*refs):
        kernel(*refs[: len(args)], *refs[len(args) + len(after) :])

    weight = WEIGHT.get(kernel.__name__, 1)
    with jax.named_scope(kernel.__name__):
        return pl.pallas_call(
            ordered,
            out_shape=[jax.ShapeDtypeStruct(s, d) for s, d in outs],
            in_specs=[SMEM]
            + [VMEM] * (len(args) - 1)
            + [pl.BlockSpec(memory_space=pl.ANY)] * len(after),
            out_specs=[VMEM] * len(outs),
            scratch_shapes=list(scratch),
            cost_estimate=pl.CostEstimate(flops=weight, bytes_accessed=weight, transcendentals=0),
            compiler_params=pltpu.CompilerParams(vmem_limit_bytes=48 * 2**20),
        )(*args, *after)


WEIGHT = {"back_kernel": 3 * 10**10}


def span(index, size):
    return pl.ds(pl.multiple_of(index * size, size), size)


def logistic(v):
    return 1.0 / (1.0 + jnp.exp(-v))


def slope(v):
    s = logistic(v)
    return s * (1.0 + v * (1.0 - s))


def split_kernel(place, images, grad, own, send):
    core = lax.rem(place[0], 2)
    rows, cols = images.shape[0], images.shape[1] // 2
    for i, x in enumerate((images, grad)):
        for r in range(rows):
            at = slice(r * cols, (r + 1) * cols)
            own[i, at, :] = x[r, span(core, cols), :]
            send[i, at, :] = x[r, span(1 - core, cols), :]


def join_kernel(place, own, got, images, grad):
    for i, out in enumerate((images, grad)):
        out[0] = own[i]
        out[1] = got[i]


def panel_kernel(place, first, third, first_got, third_got, out):
    depth, wide = first.shape
    for s, (a, b) in enumerate(((first, third), (first_got, third_got))):
        out[s, :depth, :] = a[...]
        for i in range(b.shape[1] // wide):
            at = slice(depth + i * b.shape[0], depth + (i + 1) * b.shape[0])
            out[s, at, :] = b[:, i * wide : (i + 1) * wide]


def gather_kernel(place, a0, a1, a2, a3, b0, b1, b2, b3, taps, taps_other, w1, w3, wd):
    core, chan = lax.rem(place[0], 2), place[2]
    low_z, y_here = lax.rem(chan, 2), chan // 2
    depth, half = w1.shape[1], a0.shape[2]
    mine, theirs = (a0, a1, a2, a3), (b0, b1, b2, b3)

    def fill(low, high, low_taps, high_taps):
        for step in range(4):
            y = y_here ^ step
            for s in range(2):
                k = 2 * y + (low_z ^ s)
                w1[k, :, :half] = low[step][s, :depth, :]
                w1[k, :, half:] = high[step][s, :depth, :]
                rows = span(low_z ^ s, half)
                for slot, refs in enumerate((mine, theirs)):
                    for i in range(2):
                        lanes = slice(i * half, (i + 1) * half)
                        at = slice(depth + i * half, depth + (i + 1) * half)
                        w3[y, slot, rows, lanes] = refs[step][s, at, :]
        chans = wd.shape[1]
        size = taps.shape[0] // 9
        row_group = lax.broadcasted_iota(jnp.int32, (chans, chans), 0) // size
        col_group = lax.broadcasted_iota(jnp.int32, (chans, chans), 1) // size
        keep = row_group == col_group
        both = jnp.concatenate([low_taps[...], high_taps[...]], axis=1).astype(F32)
        for t in range(9):
            whole = jnp.concatenate([both[t * size : (t + 1) * size]] * (chans // size), axis=0)
            wd[t] = jnp.where(keep, whole, 0.0).astype(BF16)

    @pl.when(core == 0)
    def _():
        fill(mine, theirs, taps, taps_other)

    @pl.when(core == 1)
    def _():
        fill(theirs, mine, taps_other, taps)


def block(place, step, slot):
    zone = lax.rem(place[0] // 2 + step, 4)
    return 2 * zone + (lax.rem(place[0], 2) ^ slot)


def outline(v, cols, top, bottom, first, last):
    rows = v.shape[0] // cols
    top[...] = v[:cols].astype(BF16)
    bottom[...] = v[(rows - 1) * cols :].astype(BF16)
    for out, c in ((first, 0), (last, cols - 1)):
        lines = [v[r * cols + c : r * cols + c + 1] for r in range(rows)]
        pad = jnp.zeros((out.shape[0] - rows - 1, v.shape[1]), F32)
        out[...] = jnp.concatenate([pad[:1]] + lines + [pad], axis=0).astype(BF16)


def first_kernel(place, own, left, right, far_a, far_b, w1, pre, act, top, bottom, first, last):
    total = None
    for step, slots in ((0, own), (3, left), (1, right), (2, (far_a, far_b))):
        for s in range(2):
            x = slots[s][...] if step == 2 else slots[s]
            v = dot(x, w1[block(place, step, s)])
            total = v if total is None else total + v
    pre[...] = total
    a = total * logistic(total)
    act[...] = a.astype(BF16)
    outline(a, top.shape[0], top, bottom, first, last)


def shifted(up, mid, down, low, high, out):
    cols, chans = up.shape
    n = mid.shape[0] + 2 * cols
    x = jnp.concatenate([up[...].astype(F32), mid[...].astype(F32), down[...].astype(F32)], axis=0)
    col = lax.rem(lax.broadcasted_iota(jnp.int32, (n, chans), 0), cols)

    def spread(edge):
        e = edge[...].astype(F32)
        parts = [jnp.broadcast_to(e[i : i + 1, :], (cols, chans)) for i in range(n // cols)]
        return jnp.concatenate(parts, axis=0)

    out[1] = x.astype(BF16)
    out[0] = jnp.where(col == 0, spread(low), pltpu.roll(x, 1, 0)).astype(BF16)
    out[2] = jnp.where(col == cols - 1, spread(high), pltpu.roll(x, n - 1, 0)).astype(BF16)


def group_kernel(place, up, mid, down, low, high, wd, pre, act, xs):
    n, cols = mid.shape[0], up.shape[0]
    shifted(up, mid, down, low, high, xs)
    total = None
    for a in range(3):
        for b in range(3):
            v = dot(xs[b, a * cols : a * cols + n, :], wd[3 * a + b])
            total = v if total is None else total + v
    pre[...] = total
    act[...] = (total * logistic(total)).astype(BF16)


def mid_kernel(place, grad, w3, p0, p1, p2a, p2b, p3):
    zone = place[0] // 2

    def part(step):
        z = lax.rem(zone + step, 4)
        return dot(grad[0], w3[z, 0], 1, 1) + dot(grad[1], w3[z, 1], 1, 1)

    half = p2a.shape[0]
    far = part(2).astype(BF16)
    p2a[...] = far[:half]
    p2b[...] = far[half:]
    p1[...] = part(1).astype(BF16)
    p3[...] = part(3).astype(BF16)
    p0[...] = part(0)


def pass_kernel(place, p1, p3, got_a, got_b, plus, minus):
    half = got_a.shape[0]
    plus[:half, :] = (p1[:half, :].astype(F32) + got_a[...].astype(F32)).astype(BF16)
    plus[half:, :] = p1[half:, :]
    minus[:half, :] = p3[:half, :]
    minus[half:, :] = (p3[half:, :].astype(F32) + got_b[...].astype(F32)).astype(BF16)


def delta_kernel(place, p0, plus, minus, pre, delta, top, bottom, first, last):
    mid = p0[...] + plus[...].astype(F32) + minus[...].astype(F32)
    d = mid * slope(pre[...])
    delta[...] = d.astype(BF16)
    outline(d, top.shape[0], top, bottom, first, last)


def back_kernel(place, up, mid, down, low, high, wd, pre, w1, fdelta, p0, p1, p2a, p2b, p3, ds):
    n, cols = mid.shape[0], up.shape[0]
    shifted(up, mid, down, low, high, ds)
    total = None
    for a in range(3):
        for b in range(3):
            at = (2 - a) * cols
            v = dot(ds[2 - b, at : at + n, :], wd[3 * a + b], 1, 1)
            total = v if total is None else total + v
    d = (total * slope(pre[...])).astype(BF16)
    fdelta[...] = d
    for s, out in ((0, p2a), (1, p2b)):
        out[...] = dot(d, w1[block(place, 2, s)], 1, 1).astype(BF16)
    for step, out in ((1, p1), (3, p3), (0, p0)):
        for s in range(2):
            v = dot(d, w1[block(place, step, s)], 1, 1)
            out[s * n : (s + 1) * n, :] = v.astype(out.dtype)


def combine_kernel(place, p0, plus, minus, keep, send):
    n = keep.shape[0]
    for s, out in ((0, keep), (1, send)):
        at = slice(s * n, (s + 1) * n)
        v = p0[at, :] + plus[at, :].astype(F32) + minus[at, :].astype(F32)
        out[...] = v.astype(out.dtype)


def merge_kernel(place, keep, got, out):
    core = lax.rem(place[0], 2)
    rows, cols = out.shape[0], out.shape[1] // 2
    for r in range(rows):
        at = slice(r * cols, (r + 1) * cols)
        out[r, span(core, cols), :] = keep[at, :]
        out[r, span(1 - core, cols), :] = got[at, :]


def merge_add_kernel(place, base, keep, got, out):
    core = lax.rem(place[0], 2)
    rows, cols = out.shape[0], out.shape[1] // 2
    for r in range(rows):
        at = slice(r * cols, (r + 1) * cols)
        for there, piece in ((span(core, cols), keep), (span(1 - core, cols), got)):
            out[r, there, :] = base[r, there, :].astype(F32) + piece[at, :].astype(F32)


def third_kernel(
    place, own, left, right, far_a, far_b, w3, grad, images, out_keep, out_send, keep, send
):
    zone = place[0] // 2
    acts = (
        (0, own[...]),
        (3, left[...]),
        (1, right[...]),
        (2, jnp.concatenate([far_a[...], far_b[...]], axis=0)),
    )
    for s, out in ((0, out_keep), (1, out_send)):
        total = images[s].astype(F32)
        third = None
        for step, a in acts:
            v = dot(a, w3[lax.rem(zone + step, 4), s])
            third = v if third is None else third + v
        out[...] = (total + third).astype(BF16)
    for step, a in acts:
        z = lax.rem(zone + step, 4)
        at = a.astype(F32).T.astype(BF16)
        size = at.shape[0]
        keep[span(z, size), :] = dot(at, grad[0])
        send[span(z, size), :] = dot(at, grad[1]).astype(BF16)


def group_grad_kernel(place, xs, delta, keep_out, send_out):
    core = lax.rem(place[0], 2)
    n, chans = delta.shape
    cols = (xs.shape[1] - n) // 2
    size = keep_out.shape[0] * 2 // 9
    wide = chans // 2
    d = delta[...]
    row_group = lax.broadcasted_iota(jnp.int32, (chans, chans), 0) // size
    col_group = lax.broadcasted_iota(jnp.int32, (chans, chans), 1) // size
    diag = row_group == col_group
    taps = []
    for t in range(9):
        a, b = t // 3, t % 3
        full = jnp.where(diag, dot(xs[b, a * cols : a * cols + n, :], d, 0, 0), 0.0)
        total = full[0:size]
        for g in range(1, chans // size):
            total += full[g * size : (g + 1) * size]
        taps.append(total)
    both = jnp.concatenate(taps, axis=0)
    half = both.shape[0] // 2
    low = jnp.concatenate([both[:half, :wide], both[half:, :wide]], axis=1)
    high = jnp.concatenate([both[:half, wide:], both[half:, wide:]], axis=1)
    keep_out[...] = jnp.where(core == 0, low, high)
    send_out[...] = jnp.where(core == 0, high, low).astype(BF16)


def first_grad_kernel(
    place, own, left, right, far_a, far_b, delta, group_keep, group_send, keep, send
):
    core = lax.rem(place[0], 2)
    d = delta[...].astype(F32).T.astype(BF16)
    rows = d.shape[0] // 2
    for step, slots in ((0, own), (3, left), (1, right), (2, (far_a, far_b))):
        for s in range(2):
            v = dot(d, slots[s][...] if step == 2 else slots[s])
            low, high = v[:rows], v[rows:]
            at = span(block(place, step, s), rows)
            keep[at, :] = jnp.where(core == 0, low, high)
            send[at, :] = jnp.where(core == 0, high, low).astype(BF16)
    keep[8 * rows :, :] = group_keep[...]
    send[8 * rows :, :] = group_send[...]


def pack_kernel(place, keep, got, third_keep, third_got, o0, o1, o2, o3):
    low_z, y_here = lax.rem(place[2], 2), place[2] // 2
    rows = third_keep.shape[0] // 8
    part = (keep[8 * rows :, :] + got[8 * rows :, :].astype(F32)).astype(BF16)
    for step, out in enumerate((o0, o1, o2, o3)):
        for s in range(2):
            at = span(2 * (y_here ^ step) + (low_z ^ s), rows)
            v = keep[at, :] + got[at, :].astype(F32)
            out[2 * s * rows : (2 * s + 1) * rows, :] = v.astype(BF16)
            v = third_keep[at, :] + third_got[at, :].astype(F32)
            out[(2 * s + 1) * rows : (2 * s + 2) * rows, :] = v.astype(BF16)
        out[4 * rows :, :] = part


def sum_y_kernel(place, a, b, c, d, out):
    v = (a[...].astype(F32) + c[...].astype(F32)) + (b[...].astype(F32) + d[...].astype(F32))
    out[...] = v.astype(BF16)


def sum_kernel(place, a, b, c, d, keep, send):
    v = (a[...].astype(F32) + c[...].astype(F32)) + (b[...].astype(F32) + d[...].astype(F32))
    keep[...] = v[: keep.shape[0]]
    send[...] = v[keep.shape[0] :].astype(BF16)


def last_kernel(place, keep, send, got, first, group, third):
    mine = keep.shape[0]
    wide = first.shape[1]
    total = keep[...] + got[:mine, :].astype(F32)
    first[...] = total[:wide].T
    third[...] = total[wide:]
    part = send[mine:, :].astype(F32) + got[mine:, :].astype(F32)
    half = group.shape[0] // 2
    group[:half, :] = part[:, :wide]
    group[half:, :] = part[:, wide:]


def body(images, first_weight, group_weight, third_weight, out_grad):
    rows_here, cols_here, chans = images.shape
    filt, chan, rows = lax.axis_size("filt"), lax.axis_size("chan"), lax.axis_size("rows")
    zones = filt // 2
    place = jnp.stack([lax.axis_index(a) for a in ("filt", "rows", "chan")]).astype(jnp.int32)
    cols = cols_here // 2
    n = rows_here * cols
    depth, own_mid = first_weight.shape
    hidden = 2 * own_mid
    pair = (2, n, chans)

    def xor(axis, k):
        return [(i, i ^ k) for i in range(lax.axis_size(axis))]

    zplus = [(z * 2 + c, (z + 1) % zones * 2 + c) for z in range(zones) for c in range(2)]
    zminus = [(t, s) for s, t in zplus]
    row_next = [(i, i + 1) for i in range(rows - 1)]
    row_prev = [(t, s) for s, t in row_next]
    col_next = [
        (k * filt + 2 * z + c, k * filt + 2 * z + 1 if c == 0 else (k + 1) * filt + 2 * z)
        for k in range(chan)
        for z in range(zones)
        for c in range(2)
        if c == 0 or k < chan - 1
    ]
    col_prev = [(t, s) for s, t in col_next]

    def swap(v):
        return lax.ppermute(v, "filt", xor("filt", 1))

    def up_z(v):
        return lax.ppermute(v, "filt", zplus)

    def down_z(v):
        return lax.ppermute(v, "filt", zminus)

    def along_y(pieces):
        return [pieces[0]] + [
            lax.ppermute(pieces[k], "chan", xor("chan", 2 * k)) for k in range(1, 4)
        ]

    def ring_scatter(p0, p1, p2a, p2b, p3, after=()):
        shape = p1.shape
        plus, minus = call(
            pass_kernel,
            [(shape, BF16)] * 2,
            (place, p1, p3, up_z(p2a), down_z(p2b)),
            after=after,
        )
        return (p0, up_z(plus), down_z(minus)), plus

    def halo(v, top, bottom, first, last):
        up = lax.ppermute(bottom, "rows", row_next)
        down = lax.ppermute(top, "rows", row_prev)

        def line(edge, c):
            end = slice(c, c + 1)
            return jnp.concatenate(
                [up[end], edge[1 : rows_here + 1], down[end], edge[rows_here + 2 :]], axis=0
            )

        low = lax.ppermute(line(last, cols - 1), ("chan", "filt"), col_next)
        high = lax.ppermute(line(first, 0), ("chan", "filt"), col_prev)
        return up, v, down, low, high

    taps = group_weight.reshape(-1, own_mid)
    beside = [lax.ppermute(w, "chan", xor("chan", 1)) for w in (first_weight, third_weight)]

    own, send = call(
        split_kernel, [(pair, BF16)] * 2, (place, images, out_grad), after=beside
    )
    img, grad = call(join_kernel, [(pair, BF16)] * 2, (place, own, swap(send)))
    left, right = up_z(img), down_z(img)
    blocks = (img, left, right, up_z(left[0]), down_z(right[1]))

    (panel,) = call(
        panel_kernel,
        [((2, depth + third_weight.size // own_mid, own_mid), BF16)],
        (place, first_weight, third_weight, *beside),
        after=(img,),
    )
    panels = along_y([panel] * 4)
    w1, w3, wd = call(
        gather_kernel,
        [
            ((chan, depth, hidden), BF16),
            ((zones, 2, hidden, chans), BF16),
            ((9, hidden, hidden), BF16),
        ],
        (place, *panels, *[swap(p) for p in panels], taps, swap(taps)),
    )

    flat = (n, hidden)
    half = (n // 2, hidden)
    mid_parts = call(
        mid_kernel,
        [(flat, F32), (flat, BF16), (half, BF16), (half, BF16), (flat, BF16)],
        (place, grad, w3),
    )
    mid_parts, passed = ring_scatter(*mid_parts)
    around = [((cols, hidden), BF16)] * 2 + [((16, hidden), BF16)] * 2
    pre_first, act_first, *edge = call(
        first_kernel,
        [(flat, F32), (flat, BF16)] + around,
        (place, *blocks, w1),
    )
    pre_group, act_group, xs = call(
        group_kernel,
        [(flat, F32), (flat, BF16), ((3, n + 2 * cols, hidden), BF16)],
        (place, *halo(act_first, *edge), wd),
        after=(passed,),
    )
    act_left, act_right = up_z(act_group), down_z(act_group)
    delta, *edge = call(
        delta_kernel, [(flat, BF16)] + around, (place, *mid_parts, pre_group)
    )
    acts = (
        act_group,
        act_left,
        act_right,
        up_z(act_left[: n // 2]),
        down_z(act_right[n // 2 :]),
    )
    two = (2 * n, chans)
    first_delta, *back_parts = call(
        back_kernel,
        [(flat, BF16), (two, F32), (two, BF16)] + [((n, chans), BF16)] * 2 + [(two, BF16)],
        (place, *halo(delta, *edge), wd, pre_first, w1),
        [pltpu.VMEM((3, n + 2 * cols, hidden), BF16)],
        after=(act_left, act_right),
    )
    group_keep, group_send = call(
        group_grad_kernel,
        [((taps.shape[0] // 2, hidden), F32), ((taps.shape[0] // 2, hidden), BF16)],
        (place, xs, delta),
    )

    out_keep, out_send, third_keep, third_send = call(
        third_kernel,
        [((n, chans), BF16)] * 2
        + [((chan * own_mid, chans), F32), ((chan * own_mid, chans), BF16)],
        (place, *acts, w3, grad, img),
        after=(first_delta,),
    )
    (block_out,) = call(
        merge_kernel, [(images.shape, BF16)], (place, out_keep, swap(out_send))
    )

    lines = own_mid + taps.shape[0] // 2
    keep, send = call(
        first_grad_kernel,
        [((lines + (chan - 1) * own_mid, chans), d) for d in (F32, BF16)],
        (place, *blocks, first_delta, group_keep, group_send),
    )
    back_parts, passed = ring_scatter(*back_parts, after=(keep, third_keep))
    lines += own_mid
    pieces = call(
        pack_kernel,
        [((lines + 2 * own_mid, chans), BF16)] * 4,
        (place, keep, swap(send), third_keep, swap(third_send)),
    )
    lined = [((lines + 2 * own_mid, chans), BF16)]
    (total,) = call(sum_y_kernel, lined, (place, *along_y(pieces)))
    others = [lax.ppermute(total, "rows", xor("rows", k)) for k in range(1, 4)]
    keep, send = call(
        sum_kernel,
        [((2 * own_mid, chans), F32), ((lines, chans), BF16)],
        (place, total, *others),
    )
    first_grad, group_grad, third_grad = call(
        last_kernel,
        [((depth, own_mid), F32), (taps.shape, F32), ((own_mid, chans), F32)],
        (place, keep, send, lax.ppermute(send, "chan", xor("chan", 1))),
    )

    keep, send = call(
        combine_kernel, [((n, chans), F32), ((n, chans), BF16)], (place, *back_parts)
    )
    (images_grad,) = call(
        merge_add_kernel, [(images.shape, F32)], (place, out_grad, keep, swap(send))
    )
    return (block_out, images_grad, first_grad, group_grad.reshape(group_weight.shape), third_grad)


def solution(mesh):
    in_specs = (
        P("rows", "chan", "filt"),
        P("chan", "filt"),
        P(None, None, None, "filt"),
        P("chan", "filt"),
        P("rows", "chan", "filt"),
    )
    out_specs = (
        P("rows", "chan", "filt"),
        P("rows", "chan", "filt"),
        P("chan", "filt"),
        P(None, None, None, "filt"),
        P("chan", "filt"),
    )
    return jax.shard_map(body, mesh=mesh, in_specs=in_specs, out_specs=out_specs, check_vma=False)
```
